32 devices in a mesh: dom: 8 (over y, x, core), rep: 4 (over z).
Axes of the slice: x: 2, y: 2, z: 4, core: 2. Of those that a mesh axis runs over, the one named last changes fastest.
Arguments:
- features: bfloat16 [32768, 512], P('dom', 'rep'), may hold values from -6 to 6
- tile_values: bfloat16 [256, 8, 128, 128], P('dom'), may hold values from -0.1875 to 0.1875
- tile_columns: int32 [256, 8], P('dom'), may hold values from 0 to 39
- boundary_rows: int32 [8, 128], P('dom'), may hold values from 0 to 4095
- train_rows: int32 [8, 4096], P('dom'), may hold values from 0 to 4095
- shuffle: int32 [8, 4096], P('dom'), may hold values from 0 to 4095, each once within a row
- labels: int32 [32768], P(('dom', 'rep')), may hold values from 0 to 152
- first_weight: bfloat16 [4, 512, 1024], replicated, may hold values from -0.125 to 0.125
- mid_weight: bfloat16 [1024, 1024], replicated, may hold values from -0.1875 to 0.1875
- out_weight: bfloat16 [1024, 153], replicated, may hold values from -0.1875 to 0.1875
Outputs:
- first_grad: float32 [4, 512, 1024], P('rep', 'dom')
- mid_grad: float32 [1024, 1024], P(('dom', 'rep'))
- out_grad: float32 [1024, 153], P(('dom', 'rep'))
The draws below stay inside these ranges and needn't reach their ends.
Inputs may be any that keep to these rules, and one draw needn't show every extreme that they name: `tile_columns`: an entry below 32 names a block of the partition's own rows, an entry c of 32 or more names block c - 32 of the gathered boundary rows. `train_rows`: indices may repeat. `shuffle`: each row is a permutation of 0 to 4095.
All inputs are finite; a program needn't handle non-finite values.
Results may differ from the reference program's by a relative error of at most 0.02.
Values may be sent and summed in bfloat16 or wider, within the bound.
A program may use at most 128 MiB of HBM per device.

```python
import math
import jax
import jax.numpy as jnp
from jax import lax

F = 512
HID = 1024
C = 153
TILE = 128
K = 8
B = 128
HOPS = 3
R = 4096
TRAIN_DEV = 4096
SLAB = 128
NB = 32
NCB = 40
NODES = 32768
TRAIN = 32768
GROUP = 512
N_DOM = 8
N_REP = 4


def place_ends(entries, rng, least, top_value):
    spot = [jax.random.randint(jax.random.fold_in(rng, axis), (), 0, length) for axis, length in enumerate(entries.shape)]
    longest = entries.shape.index(max(entries.shape))
    beside = spot[:longest] + [(spot[longest] + 1) % entries.shape[longest]] + spot[longest + 1:]
    return entries.at[tuple(spot)].set(least).at[tuple(beside)].set(top_value)


def steps_of(stream_key, dims, cuts, least, top_value):
    def one(axis_at, blocks):
        heights = jax.random.uniform(jax.random.fold_in(jax.random.fold_in(stream_key, 6), axis_at), (blocks,), jnp.float32, least / len(cuts), top_value / len(cuts))
        return jnp.repeat(jnp.exp(heights), dims[axis_at] // blocks).reshape((-1,) + (1,) * (len(dims) - axis_at - 1))

    factor_of = one(*cuts[0])
    for cut in cuts[1:]:
        factor_of = factor_of * one(*cut)
    return factor_of


def centred(own_key, shape, deviation, limit, cuts=(), held_as=jnp.bfloat16):
    drawn = deviation * jax.random.normal(own_key, shape, jnp.float32)
    if cuts:
        drawn = drawn * steps_of(own_key, shape, cuts, -0.22, 0.18)
    return jnp.clip(drawn, -limit, limit).astype(held_as)


def setup_inputs(seed: int = 0) -> dict:
    streams_of = jax.random.split(jax.random.key(seed), 11)
    return {
        "features": centred(streams_of[0], (NODES, F), 1.0, 6.0, ((0, 8), (1, 4))),
        "tile_values": centred(streams_of[1], (N_DOM * NB, K, TILE, TILE), (K * TILE) ** -0.5, 0.1875, ((0, 8),)),
        "tile_columns": place_ends(jax.random.randint(streams_of[2], (N_DOM * NB, K), 0, NCB), jax.random.fold_in(streams_of[2], 1), 0, NCB - 1).astype(jnp.int32),
        "boundary_rows": place_ends(jax.random.randint(streams_of[3], (N_DOM, B), 0, R), jax.random.fold_in(streams_of[3], 1), 0, R - 1).astype(jnp.int32),
        "train_rows": place_ends(jax.random.randint(streams_of[4], (N_DOM, TRAIN_DEV), 0, R), jax.random.fold_in(streams_of[4], 1), 0, R - 1).astype(jnp.int32),
        "shuffle": jax.vmap(lambda own: jax.random.permutation(own, TRAIN_DEV))(jax.random.split(streams_of[5], N_DOM)).reshape((N_DOM, TRAIN_DEV)).astype(jnp.int32),
        "labels": place_ends(jax.random.randint(streams_of[6], (TRAIN,), 0, C), jax.random.fold_in(streams_of[6], 1), 0, C - 1).astype(jnp.int32),
        "first_weight": centred(streams_of[7], (N_REP, (HOPS + 1) * SLAB, HID), ((HOPS + 1) * F) ** -0.5, 0.125),
        "mid_weight": centred(streams_of[8], (HID, HID), HID ** -0.5, 0.1875),
        "out_weight": centred(streams_of[9], (HID, C), HID ** -0.5, 0.1875),
    }


root_two_pi = 0.7978845608028654
cubic_term = 0.044715

def gelu_pair(values):
    inner_arg = root_two_pi * (values + cubic_term * values * values * values)
    tanh_part = jnp.tanh(inner_arg)
    output = 0.5 * values * (1.0 + tanh_part)
    slope_out = 0.5 * (1.0 + tanh_part) + 0.5 * values * (1.0 - tanh_part * tanh_part) * root_two_pi * (1.0 + 3.0 * cubic_term * values * values)
    return (output, slope_out)

def outer_rows(left_side, right_side):
    return lax.dot_general(left_side, right_side, (((0,), (0,)), ((), ())), preferred_element_type=jnp.float32)

def inner_cols(left_side, right_side):
    return lax.dot_general(left_side, right_side, (((1,), (1,)), ((), ())), preferred_element_type=jnp.float32)

def reference(features, tile_values, tile_columns, boundary_rows, train_rows, shuffle, labels, first_weight, mid_weight, out_weight):
    tiles = tile_values.reshape(N_DOM, NB, K, TILE, TILE)
    columns = tile_columns.reshape(N_DOM, NB, K)
    offsets = (jnp.arange(N_DOM, dtype=jnp.int32) * R)[:, None]
    halo_index = (boundary_rows + offsets).reshape(-1)
    hop_list = [features]
    for hop_index in range(HOPS):
        current = hop_list[-1]
        halo_rows = current[halo_index]
        own_parts = current.reshape(N_DOM, R, F)

        def one_part(pieces):
            own_rows, part_tiles, part_columns = pieces
            joined = jnp.concatenate([own_rows, halo_rows], axis=0)
            blocks = joined.reshape(NCB, TILE, F)
            picked = blocks[part_columns]
            summed = jnp.einsum('bkij,bkjf->bif', part_tiles.astype(jnp.float32), picked.astype(jnp.float32))
            return summed.reshape(R, F).astype(jnp.bfloat16)
        hop_list.append(lax.map(one_part, (own_parts, tiles, columns)).reshape(NODES, F))
    local_pick = jnp.take_along_axis(train_rows, shuffle, axis=1) + offsets
    selected = local_pick.reshape(N_DOM, N_DOM, GROUP).transpose(1, 0, 2).reshape(-1)
    stacked = jnp.stack([hop[selected] for hop in hop_list], axis=1)
    inputs = stacked.reshape(TRAIN, HOPS + 1, N_REP, SLAB).transpose(0, 2, 1, 3).reshape(TRAIN, (HOPS + 1) * F)
    pre_first = jnp.dot(inputs, first_weight.reshape((HOPS + 1) * F, HID), preferred_element_type=jnp.float32)
    act_first, slope_first = gelu_pair(pre_first)
    act_first = act_first.astype(jnp.bfloat16)
    pre_mid = jnp.dot(act_first, mid_weight, preferred_element_type=jnp.float32)
    act_mid, slope_mid = gelu_pair(pre_mid)
    act_mid = act_mid.astype(jnp.bfloat16)
    logits = jnp.dot(act_mid, out_weight, preferred_element_type=jnp.float32)
    exp_logits = jnp.exp(logits)
    softmax_out = exp_logits / lax.optimization_barrier(jnp.sum(exp_logits, axis=1, keepdims=True))
    onehot = (labels[:, None] == jnp.arange(C, dtype=jnp.int32)[None, :]).astype(jnp.float32)
    grad_logits = ((softmax_out - onehot) * (1.0 / math.sqrt(TRAIN))).astype(jnp.bfloat16)
    grad_mid = (inner_cols(grad_logits, out_weight) * slope_mid).astype(jnp.bfloat16)
    grad_first = (inner_cols(grad_mid, mid_weight) * slope_first).astype(jnp.bfloat16)
    out_grad = outer_rows(act_mid, grad_logits)
    mid_grad = outer_rows(act_first, grad_mid)
    first_grad = outer_rows(inputs, grad_first).reshape(N_REP, (HOPS + 1) * SLAB, HID)
    return (first_grad, mid_grad, out_grad)
```

```python
import functools
import math

import jax
import jax.numpy as jnp
from jax import lax
from jax.experimental import pallas as pl
from jax.experimental.pallas import tpu as pltpu
from jax.sharding import PartitionSpec as P

HOPS = 3
STEP_BLOCKS = 8

root_two_pi = 0.7978845608028654
cubic_term = 0.044715


def gelu_pair(values):
    inner_arg = root_two_pi * (values + cubic_term * values * values * values)
    tanh_part = jnp.tanh(inner_arg)
    output = 0.5 * values * (1.0 + tanh_part)
    slope_out = 0.5 * (1.0 + tanh_part) + 0.5 * values * (
        1.0 - tanh_part * tanh_part
    ) * root_two_pi * (1.0 + 3.0 * cubic_term * values * values)
    return (output, slope_out)


def outer_rows(left_side, right_side):
    return lax.dot_general(
        left_side, right_side, (((0,), (0,)), ((), ())), preferred_element_type=jnp.float32
    )


def inner_cols(left_side, right_side):
    return lax.dot_general(
        left_side, right_side, (((1,), (1,)), ((), ())), preferred_element_type=jnp.float32
    )


def hop_kernel(columns, hop_ref, halo_ref, tiles_ref, pick_ref, out_ref, export_ref, joined, total):
    step = pl.program_id(0)
    own_rows = hop_ref.shape[0]
    _, fan_in, tile, _ = tiles_ref.shape

    @pl.when(step == 0)
    def _():
        joined[:own_rows] = hop_ref[...]
        joined[own_rows:] = halo_ref[...]
        total[...] = jnp.zeros_like(total)

    for block in range(STEP_BLOCKS):
        row = step * STEP_BLOCKS + block
        left = jnp.concatenate([tiles_ref[block, k] for k in range(fan_in)], axis=1)
        right = jnp.concatenate(
            [
                joined[pl.ds(pl.multiple_of(columns[row, k] * tile, tile), tile)]
                for k in range(fan_in)
            ],
            axis=0,
        )
        summed = jnp.dot(left, right, preferred_element_type=jnp.float32)
        out_ref[block * tile : (block + 1) * tile] = summed.astype(out_ref.dtype)
    total[...] += jnp.dot(pick_ref[...], out_ref[...], preferred_element_type=jnp.float32)

    @pl.when(step == pl.num_programs(0) - 1)
    def _():
        export_ref[...] = total[...].astype(export_ref.dtype)


def propagate(hop_now, halo_rows, tile_columns, tile_values, pick_boundary):
    rows, width = hop_now.shape
    blocks, fan_in, tile, _ = tile_values.shape
    exported = pick_boundary.shape[0]
    step_rows = STEP_BLOCKS * tile
    whole = lambda step, columns: (0, 0)
    return pl.pallas_call(
        hop_kernel,
        grid_spec=pltpu.PrefetchScalarGridSpec(
            num_scalar_prefetch=1,
            grid=(blocks // STEP_BLOCKS,),
            in_specs=[
                pl.BlockSpec((rows, width), whole),
                pl.BlockSpec(halo_rows.shape, whole),
                pl.BlockSpec(
                    (STEP_BLOCKS, fan_in, tile, tile), lambda step, columns: (step, 0, 0, 0)
                ),
                pl.BlockSpec((exported, step_rows), lambda step, columns: (0, step)),
            ],
            out_specs=[
                pl.BlockSpec((step_rows, width), lambda step, columns: (step, 0)),
                pl.BlockSpec((exported, width), whole),
            ],
            scratch_shapes=[
                pltpu.VMEM((rows + halo_rows.shape[0], width), jnp.bfloat16),
                pltpu.VMEM((exported, width), jnp.float32),
            ],
        ),
        out_shape=[
            jax.ShapeDtypeStruct((rows, width), jnp.bfloat16),
            jax.ShapeDtypeStruct((exported, width), jnp.bfloat16),
        ],
        compiler_params=pltpu.CompilerParams(vmem_limit_bytes=40 * 1024 * 1024),
        cost_estimate=pl.CostEstimate(
            flops=2 * blocks * fan_in * tile * tile * width,
            bytes_accessed=2 * (tile_values.size + 4 * rows * width),
            transcendentals=0,
        ),
        name="propagate_hop",
    )(tile_columns, hop_now, halo_rows, tile_values, pick_boundary)


def to_rows(hop_now, n_rep):
    rows, width = hop_now.shape
    sent = hop_now.reshape(n_rep, rows // n_rep, width)
    return lax.all_to_all(sent, "rep", split_axis=0, concat_axis=0, tiled=True)


def per_device(
    features,
    tile_values,
    tile_columns,
    boundary_rows,
    train_rows,
    shuffle,
    labels,
    first_weight,
    mid_weight,
    out_weight,
):
    n_dom = lax.axis_size("dom")
    n_rep = lax.axis_size("rep")
    rows, width = features.shape
    train_dev = shuffle.shape[1]
    batch_rows = rows // n_rep
    hidden = mid_weight.shape[0]
    classes = out_weight.shape[1]
    hop_count = HOPS + 1

    bound = boundary_rows[0]
    pick_boundary = (bound[:, None] == jnp.arange(rows, dtype=jnp.int32)[None, :]).astype(
        jnp.bfloat16
    )

    hop_now = features
    exported = features[bound]
    moved = [to_rows(hop_now, n_rep)]
    for hop_index in range(HOPS):
        halo_rows = lax.all_gather(exported, "dom", axis=0, tiled=True)
        hop_now, exported = propagate(
            hop_now, halo_rows, tile_columns, tile_values, pick_boundary
        )
        moved.append(to_rows(hop_now, n_rep))

    all_labels = lax.all_gather(labels, ("dom", "rep"), axis=0, tiled=True)
    own_labels = lax.dynamic_index_in_dim(
        all_labels.reshape(n_dom, n_dom, train_dev // n_dom),
        lax.axis_index("dom"),
        axis=1,
        keepdims=False,
    ).reshape(train_dev)
    picked_rows = train_rows[0][shuffle[0]] - lax.axis_index("rep") * batch_rows
    paper_hot = (
        picked_rows[:, None] == jnp.arange(batch_rows, dtype=jnp.int32)[None, :]
    ).astype(jnp.bfloat16)
    label_hot = (own_labels[:, None] == jnp.arange(classes, dtype=jnp.int32)[None, :]).astype(
        jnp.bfloat16
    )
    counts = outer_rows(paper_hot, label_hot)
    times = jnp.sum(counts, axis=1, keepdims=True)

    pre_first = None
    columns = []
    for hop_index in range(hop_count):
        part = moved[hop_index].transpose(1, 0, 2).reshape(batch_rows, n_rep * width)
        columns.append(part)
        weight = first_weight[:, hop_index * width : (hop_index + 1) * width].reshape(
            n_rep * width, hidden
        )
        term = jnp.dot(part, weight, preferred_element_type=jnp.float32)
        pre_first = term if pre_first is None else pre_first + term
    act_first, slope_first = gelu_pair(pre_first)
    act_first = act_first.astype(jnp.bfloat16)
    pre_mid = jnp.dot(act_first, mid_weight, preferred_element_type=jnp.float32)
    act_mid, slope_mid = gelu_pair(pre_mid)
    act_mid = act_mid.astype(jnp.bfloat16)
    logits = jnp.dot(act_mid, out_weight, preferred_element_type=jnp.float32)
    exp_logits = jnp.exp(logits)
    softmax_out = exp_logits / jnp.sum(exp_logits, axis=1, keepdims=True)
    grad_logits = jnp.where(times > 0.0, softmax_out * times - counts, 0.0)
    grad_logits = (grad_logits * (1.0 / math.sqrt(n_dom * train_dev))).astype(jnp.bfloat16)
    grad_mid = (inner_cols(grad_logits, out_weight) * slope_mid).astype(jnp.bfloat16)

    def share(full, lead):
        part = lax.psum_scatter(full, "dom", scatter_dimension=lead, tiled=True)
        return lax.psum_scatter(part, "rep", scatter_dimension=0, tiled=True)

    out_share = outer_rows(act_mid, grad_logits).astype(jnp.bfloat16)
    out_share = out_share.reshape(n_dom, n_rep, hidden // (n_dom * n_rep), classes)
    out_share = lax.psum_scatter(out_share, "dom", scatter_dimension=0, tiled=False)
    out_share = lax.psum_scatter(out_share, "rep", scatter_dimension=0, tiled=False)
    mid_share = outer_rows(act_first, grad_mid).astype(jnp.bfloat16)
    mid_share = mid_share.reshape(n_dom, n_rep, hidden // (n_dom * n_rep), hidden)
    mid_share = lax.psum_scatter(mid_share, "dom", scatter_dimension=0, tiled=False)
    mid_share = lax.psum_scatter(mid_share, "rep", scatter_dimension=0, tiled=False)

    grad_first = (inner_cols(grad_mid, mid_weight) * slope_first).astype(jnp.bfloat16)
    first_parts = [
        outer_rows(part, grad_first).astype(jnp.bfloat16).reshape(n_rep, width, hidden)
        for part in columns
    ]
    first_share = jnp.concatenate(first_parts, axis=1)
    quarter = hop_count * width // n_dom
    first_share = share(first_share, 1)
    return (
        first_share.astype(jnp.float32).reshape(1, quarter, hidden),
        mid_share.astype(jnp.float32),
        out_share.astype(jnp.float32),
    )


def solution(mesh):
    placed = (
        P("dom", "rep"),
        P("dom", None, None, None),
        P("dom", None),
        P("dom", None),
        P("dom", None),
        P("dom", None),
        P(("dom", "rep")),
        P(),
        P(),
        P(),
    )
    return jax.shard_map(
        per_device,
        mesh=mesh,
        in_specs=placed,
        out_specs=(P("rep", "dom", None), P(("dom", "rep"), None), P(("dom", "rep"), None)),
        check_vma=False,
    )
```

```python
import functools
import math

import jax
import jax.numpy as jnp
from jax import lax
from jax.experimental import pallas as pl
from jax.experimental.pallas import tpu as pltpu
from jax.sharding import PartitionSpec as P

HOPS = 3
STEP_BLOCKS = 8

root_two_pi = 0.7978845608028654
cubic_term = 0.044715


def gelu_pair(values):
    inner_arg = root_two_pi * (values + cubic_term * values * values * values)
    tanh_part = jnp.tanh(inner_arg)
    output = 0.5 * values * (1.0 + tanh_part)
    slope_out = 0.5 * (1.0 + tanh_part) + 0.5 * values * (
        1.0 - tanh_part * tanh_part
    ) * root_two_pi * (1.0 + 3.0 * cubic_term * values * values)
    return (output, slope_out)


def outer_rows(left_side, right_side):
    return lax.dot_general(
        left_side, right_side, (((0,), (0,)), ((), ())), preferred_element_type=jnp.float32
    )


def inner_cols(left_side, right_side):
    return lax.dot_general(
        left_side, right_side, (((1,), (1,)), ((), ())), preferred_element_type=jnp.float32
    )


def hop_kernel(columns, hop_ref, halo_ref, tiles_ref, pick_ref, out_ref, export_ref, joined, total):
    step = pl.program_id(0)
    own_rows = hop_ref.shape[0]
    _, fan_in, tile, _ = tiles_ref.shape

    @pl.when(step == 0)
    def _():
        joined[:own_rows] = hop_ref[...]
        joined[own_rows:] = halo_ref[...]
        total[...] = jnp.zeros_like(total)

    for block in range(STEP_BLOCKS):
        row = step * STEP_BLOCKS + block
        left = jnp.concatenate([tiles_ref[block, k] for k in range(fan_in)], axis=1)
        right = jnp.concatenate(
            [
                joined[pl.ds(pl.multiple_of(columns[row, k] * tile, tile), tile)]
                for k in range(fan_in)
            ],
            axis=0,
        )
        summed = jnp.dot(left, right, preferred_element_type=jnp.float32)
        out_ref[block * tile : (block + 1) * tile] = summed.astype(out_ref.dtype)
    total[...] += jnp.dot(pick_ref[...], out_ref[...], preferred_element_type=jnp.float32)

    @pl.when(step == pl.num_programs(0) - 1)
    def _():
        export_ref[...] = total[...].astype(export_ref.dtype)


def propagate(hop_now, halo_rows, tile_columns, tile_values, pick_boundary):
    rows, width = hop_now.shape
    blocks, fan_in, tile, _ = tile_values.shape
    exported = pick_boundary.shape[0]
    step_rows = STEP_BLOCKS * tile
    whole = lambda step, columns: (0, 0)
    return pl.pallas_call(
        hop_kernel,
        grid_spec=pltpu.PrefetchScalarGridSpec(
            num_scalar_prefetch=1,
            grid=(blocks // STEP_BLOCKS,),
            in_specs=[
                pl.BlockSpec((rows, width), whole),
                pl.BlockSpec(halo_rows.shape, whole),
                pl.BlockSpec(
                    (STEP_BLOCKS, fan_in, tile, tile), lambda step, columns: (step, 0, 0, 0)
                ),
                pl.BlockSpec((exported, step_rows), lambda step, columns: (0, step)),
            ],
            out_specs=[
                pl.BlockSpec((step_rows, width), lambda step, columns: (step, 0)),
                pl.BlockSpec((exported, width), whole),
            ],
            scratch_shapes=[
                pltpu.VMEM((rows + halo_rows.shape[0], width), jnp.bfloat16),
                pltpu.VMEM((exported, width), jnp.float32),
            ],
        ),
        out_shape=[
            jax.ShapeDtypeStruct((rows, width), jnp.bfloat16),
            jax.ShapeDtypeStruct((exported, width), jnp.bfloat16),
        ],
        compiler_params=pltpu.CompilerParams(vmem_limit_bytes=40 * 1024 * 1024),
        cost_estimate=pl.CostEstimate(
            flops=2 * blocks * fan_in * tile * tile * width,
            bytes_accessed=2 * (tile_values.size + 4 * rows * width),
            transcendentals=0,
        ),
        name="propagate_hop",
    )(tile_columns, hop_now, halo_rows, tile_values, pick_boundary)


def exchange_rows(sent):
    return lax.all_to_all(sent, "rep", split_axis=0, concat_axis=0, tiled=True)


def halve(part, name, bit, axis):
    size = lax.axis_size(name)
    mine = (lax.axis_index(name) >> bit) & 1
    kept = lax.dynamic_index_in_dim(part, mine, axis, keepdims=False)
    sent = lax.dynamic_index_in_dim(part, 1 - mine, axis, keepdims=False)
    pairs = [(i, i ^ (1 << bit)) for i in range(size)]
    came = lax.ppermute(sent, name, pairs)
    return kept.astype(jnp.float32) + came.astype(jnp.float32)


def scatter_sum(part, bits, order):
    rows, cols = part.shape[-2:]
    left = list(bits)
    for bit in order:
        axis = 1 + left.index(bit)
        part = halve(part, "dom", bit, axis).astype(jnp.bfloat16)
        left.remove(bit)
    rep_bits = part.shape[0].bit_length() - 1
    part = part.reshape((2,) * rep_bits + (rows, cols))
    for bit in range(rep_bits):
        part = part.astype(jnp.bfloat16)
        part = halve(part, "rep", bit, rep_bits - 1 - bit)
    return part


def scatter_two_ways(part, dom_bits):
    n_rep, _, rows, cols = part.shape
    bits = list(range(dom_bits - 1, 0, -1))
    part = part.reshape((n_rep,) + (2,) * len(bits) + (rows, cols))
    rest = bits[::-1]
    middle = len(rest) // 2
    shares = [
        scatter_sum(part[..., : cols // 2], bits, rest),
        scatter_sum(part[..., cols // 2 :], bits, rest[middle:] + rest[:middle]),
    ]
    return jnp.concatenate(shares, axis=-1)


def per_device(
    features,
    tile_values,
    tile_columns,
    boundary_rows,
    train_rows,
    shuffle,
    labels,
    first_weight,
    mid_weight,
    out_weight,
):
    n_dom = lax.axis_size("dom")
    n_rep = lax.axis_size("rep")
    rows, width = features.shape
    train_dev = shuffle.shape[1]
    batch_rows = rows // n_rep
    hidden = mid_weight.shape[0]
    classes = out_weight.shape[1]
    hop_count = HOPS + 1

    bound = boundary_rows[0]
    pick_boundary = (bound[:, None] == jnp.arange(rows, dtype=jnp.int32)[None, :]).astype(
        jnp.bfloat16
    )

    label_rows = labels.astype(jnp.bfloat16).reshape(-1, width)
    lines = label_rows.shape[0]
    label_rows = jnp.concatenate([label_rows, label_rows], axis=0)
    riders = jnp.broadcast_to(label_rows[None], (n_rep,) + label_rows.shape)
    hop_now = features
    exported = features[bound]
    first_rows = exchange_rows(
        jnp.concatenate([hop_now.reshape(n_rep, batch_rows, width), riders], axis=1)
    )
    moved = [first_rows[:, :batch_rows]]
    part_labels = first_rows[:, batch_rows : batch_rows + lines].reshape(n_rep * lines, width)
    borders = bound.shape[0]
    for hop_index in range(HOPS):
        if hop_index == HOPS - 1:
            gathered = lax.all_gather(jnp.concatenate([exported, part_labels], axis=0), "dom")
            halo_rows = gathered[:, :borders].reshape(n_dom * borders, width)
            all_labels = gathered[:, borders:]
        else:
            halo_rows = lax.all_gather(exported, "dom", axis=0, tiled=True)
        hop_now, exported = propagate(
            hop_now, halo_rows, tile_columns, tile_values, pick_boundary
        )
        moved.append(exchange_rows(hop_now.reshape(n_rep, batch_rows, width)))

    own_labels = lax.dynamic_index_in_dim(
        all_labels.reshape(n_dom, n_dom, train_dev // n_dom),
        lax.axis_index("dom"),
        axis=1,
        keepdims=False,
    ).reshape(train_dev).astype(jnp.int32)
    picked_rows = train_rows[0][shuffle[0]] - lax.axis_index("rep") * batch_rows
    paper_hot = (
        picked_rows[:, None] == jnp.arange(batch_rows, dtype=jnp.int32)[None, :]
    ).astype(jnp.bfloat16)
    label_hot = (own_labels[:, None] == jnp.arange(classes, dtype=jnp.int32)[None, :]).astype(
        jnp.bfloat16
    )
    counts = outer_rows(paper_hot, label_hot)
    times = jnp.sum(counts, axis=1, keepdims=True)

    pre_first = None
    columns = []
    for hop_index in range(hop_count):
        part = moved[hop_index].transpose(1, 0, 2).reshape(batch_rows, n_rep * width)
        columns.append(part)
        weight = first_weight[:, hop_index * width : (hop_index + 1) * width].reshape(
            n_rep * width, hidden
        )
        term = jnp.dot(part, weight, preferred_element_type=jnp.float32)
        pre_first = term if pre_first is None else pre_first + term
    act_first, slope_first = gelu_pair(pre_first)
    act_first = act_first.astype(jnp.bfloat16)
    pre_mid = jnp.dot(act_first, mid_weight, preferred_element_type=jnp.float32)
    act_mid, slope_mid = gelu_pair(pre_mid)
    act_mid = act_mid.astype(jnp.bfloat16)
    logits = jnp.dot(act_mid, out_weight, preferred_element_type=jnp.float32)
    exp_logits = jnp.exp(logits)
    softmax_out = exp_logits / jnp.sum(exp_logits, axis=1, keepdims=True)
    grad_logits = jnp.where(times > 0.0, softmax_out * times - counts, 0.0)
    grad_logits = (grad_logits * (1.0 / math.sqrt(n_dom * train_dev))).astype(jnp.bfloat16)
    grad_mid = (inner_cols(grad_logits, out_weight) * slope_mid).astype(jnp.bfloat16)

    dom_bits = n_dom.bit_length() - 1
    quarter = hop_count * width // n_dom
    strip = hidden // (n_dom * n_rep)

    out_share = outer_rows(act_mid, grad_logits).astype(jnp.bfloat16)
    out_pad = -classes % 256
    out_share = jnp.pad(out_share, ((0, 0), (0, out_pad)))
    mid_share = outer_rows(act_first, grad_mid).astype(jnp.bfloat16)
    upper = jnp.concatenate([mid_share, out_share], axis=1)
    upper = upper.reshape(n_dom // 2, 2, n_rep, strip, hidden + classes + out_pad)
    upper = halve(upper, "dom", 0, 1).astype(jnp.bfloat16)
    upper = scatter_two_ways(upper.transpose(1, 0, 2, 3), dom_bits)

    grad_first = (inner_cols(grad_mid, mid_weight) * slope_first).astype(jnp.bfloat16)
    first_parts = []
    for part in columns:
        piece = outer_rows(part, grad_first).astype(jnp.bfloat16)
        piece = piece.reshape(n_rep, n_dom // (2 * hop_count), 2, quarter, hidden)
        first_parts.append(halve(piece, "dom", 0, 2).astype(jnp.bfloat16))
    lower = scatter_two_ways(jnp.concatenate(first_parts, axis=1), dom_bits)
    return (
        lower.reshape(1, quarter, hidden),
        upper[:, :hidden],
        upper[:, hidden : hidden + classes],
    )


def solution(mesh):
    placed = (
        P("dom", "rep"),
        P("dom", None, None, None),
        P("dom", None),
        P("dom", None),
        P("dom", None),
        P("dom", None),
        P(("dom", "rep")),
        P(),
        P(),
        P(),
    )
    return jax.shard_map(
        per_device,
        mesh=mesh,
        in_specs=placed,
        out_specs=(P("rep", "dom", None), P(("dom", "rep"), None), P(("dom", "rep"), None)),
        check_vma=False,
    )
```

```python
import functools
import math

import jax
import jax.numpy as jnp
from jax import lax
from jax.experimental import pallas as pl
from jax.experimental.pallas import tpu as pltpu
from jax.sharding import PartitionSpec as P

HOPS = 3
STEP_BLOCKS = 8

root_two_pi = 0.7978845608028654
cubic_term = 0.044715


def gelu_pair(values):
    inner_arg = root_two_pi * (values + cubic_term * values * values * values)
    tanh_part = jnp.tanh(inner_arg)
    output = 0.5 * values * (1.0 + tanh_part)
    slope_out = 0.5 * (1.0 + tanh_part) + 0.5 * values * (
        1.0 - tanh_part * tanh_part
    ) * root_two_pi * (1.0 + 3.0 * cubic_term * values * values)
    return (output, slope_out)


def outer_rows(left_side, right_side):
    return lax.dot_general(
        left_side, right_side, (((0,), (0,)), ((), ())), preferred_element_type=jnp.float32
    )


def inner_cols(left_side, right_side):
    return lax.dot_general(
        left_side, right_side, (((1,), (1,)), ((), ())), preferred_element_type=jnp.float32
    )


def hop_kernel(columns, hop_ref, halo_ref, tiles_ref, pick_ref, out_ref, export_ref, joined, total):
    step = pl.program_id(0)
    own_rows = hop_ref.shape[0]
    _, fan_in, tile, _ = tiles_ref.shape

    @pl.when(step == 0)
    def _():
        joined[:own_rows] = hop_ref[...]
        joined[own_rows:] = halo_ref[...]
        total[...] = jnp.zeros_like(total)

    for block in range(STEP_BLOCKS):
        row = step * STEP_BLOCKS + block
        left = jnp.concatenate([tiles_ref[block, k] for k in range(fan_in)], axis=1)
        right = jnp.concatenate(
            [
                joined[pl.ds(pl.multiple_of(columns[row, k] * tile, tile), tile)]
                for k in range(fan_in)
            ],
            axis=0,
        )
        summed = jnp.dot(left, right, preferred_element_type=jnp.float32)
        out_ref[block * tile : (block + 1) * tile] = summed.astype(out_ref.dtype)
    total[...] += jnp.dot(pick_ref[...], out_ref[...], preferred_element_type=jnp.float32)

    @pl.when(step == pl.num_programs(0) - 1)
    def _():
        export_ref[...] = total[...].astype(export_ref.dtype)


def propagate(hop_now, halo_rows, tile_columns, tile_values, pick_boundary):
    rows, width = hop_now.shape
    blocks, fan_in, tile, _ = tile_values.shape
    exported = pick_boundary.shape[0]
    step_rows = STEP_BLOCKS * tile
    whole = lambda step, columns: (0, 0)
    return pl.pallas_call(
        hop_kernel,
        grid_spec=pltpu.PrefetchScalarGridSpec(
            num_scalar_prefetch=1,
            grid=(blocks // STEP_BLOCKS,),
            in_specs=[
                pl.BlockSpec((rows, width), whole),
                pl.BlockSpec(halo_rows.shape, whole),
                pl.BlockSpec(
                    (STEP_BLOCKS, fan_in, tile, tile), lambda step, columns: (step, 0, 0, 0)
                ),
                pl.BlockSpec((exported, step_rows), lambda step, columns: (0, step)),
            ],
            out_specs=[
                pl.BlockSpec((step_rows, width), lambda step, columns: (step, 0)),
                pl.BlockSpec((exported, width), whole),
            ],
            scratch_shapes=[
                pltpu.VMEM((rows + halo_rows.shape[0], width), jnp.bfloat16),
                pltpu.VMEM((exported, width), jnp.float32),
            ],
        ),
        out_shape=[
            jax.ShapeDtypeStruct((rows, width), jnp.bfloat16),
            jax.ShapeDtypeStruct((exported, width), jnp.bfloat16),
        ],
        compiler_params=pltpu.CompilerParams(vmem_limit_bytes=40 * 1024 * 1024),
        cost_estimate=pl.CostEstimate(
            flops=2 * blocks * fan_in * tile * tile * width,
            bytes_accessed=2 * (tile_values.size + 4 * rows * width),
            transcendentals=0,
        ),
        name="propagate_hop",
    )(tile_columns, hop_now, halo_rows, tile_values, pick_boundary)


def exchange_rows(sent):
    return lax.all_to_all(sent, "rep", split_axis=0, concat_axis=0, tiled=True)


def halve(part, name, bit, axis):
    size = lax.axis_size(name)
    mine = (lax.axis_index(name) >> bit) & 1
    kept = lax.dynamic_index_in_dim(part, mine, axis, keepdims=False)
    sent = lax.dynamic_index_in_dim(part, 1 - mine, axis, keepdims=False)
    pairs = [(i, i ^ (1 << bit)) for i in range(size)]
    came = lax.ppermute(sent, name, pairs)
    return kept.astype(jnp.float32) + came.astype(jnp.float32)


def scatter_sum(part, bits, order):
    rows, cols = part.shape[-2:]
    left = list(bits)
    for bit in order:
        axis = 1 + left.index(bit)
        part = halve(part, "dom", bit, axis).astype(jnp.bfloat16)
        left.remove(bit)
    rep_bits = part.shape[0].bit_length() - 1
    part = part.reshape((2,) * rep_bits + (rows, cols))
    for bit in range(rep_bits):
        part = part.astype(jnp.bfloat16)
        part = halve(part, "rep", bit, rep_bits - 1 - bit)
    return part


def scatter_two_ways(part, dom_bits):
    n_rep, _, rows, cols = part.shape
    bits = list(range(dom_bits - 1, 0, -1))
    part = part.reshape((n_rep,) + (2,) * len(bits) + (rows, cols))
    rest = bits[::-1]
    middle = len(rest) // 2
    shares = [
        scatter_sum(part[..., : cols // 2], bits, rest),
        scatter_sum(part[..., cols // 2 :], bits, rest[middle:] + rest[:middle]),
    ]
    return jnp.concatenate(shares, axis=-1)


def look_up(table, places):
    side = 64
    cells = table.reshape(-1, side)
    parts = jnp.concatenate([cells // side, cells % side], axis=1).astype(jnp.bfloat16)
    lines = jnp.arange(cells.shape[0], dtype=jnp.int32)
    line_hot = ((places // side)[:, None] == lines[None, :]).astype(jnp.bfloat16)
    found = jnp.dot(line_hot, parts, preferred_element_type=jnp.float32)
    found = found[:, :side] * side + found[:, side:]
    own = (places % side)[:, None] == jnp.arange(side, dtype=jnp.int32)[None, :]
    return jnp.sum(jnp.where(own, found, 0.0), axis=1, keepdims=True).astype(jnp.int32)


def per_device(
    features,
    tile_values,
    tile_columns,
    boundary_rows,
    train_rows,
    shuffle,
    labels,
    first_weight,
    mid_weight,
    out_weight,
):
    n_dom = lax.axis_size("dom")
    n_rep = lax.axis_size("rep")
    rows, width = features.shape
    train_dev = shuffle.shape[1]
    batch_rows = rows // n_rep
    hidden = mid_weight.shape[0]
    classes = out_weight.shape[1]
    hop_count = HOPS + 1

    bound = boundary_rows[0]
    pick_boundary = (bound[:, None] == jnp.arange(rows, dtype=jnp.int32)[None, :]).astype(
        jnp.bfloat16
    )

    label_rows = labels.astype(jnp.bfloat16).reshape(-1, width)
    lines = label_rows.shape[0]
    label_rows = jnp.concatenate([label_rows, label_rows], axis=0)
    riders = jnp.broadcast_to(label_rows[None], (n_rep,) + label_rows.shape)
    hop_now = features
    exported = features[bound]
    first_rows = exchange_rows(
        jnp.concatenate([hop_now.reshape(n_rep, batch_rows, width), riders], axis=1)
    )
    moved = [first_rows[:, :batch_rows]]
    part_labels = first_rows[:, batch_rows : batch_rows + lines].reshape(n_rep * lines, width)
    borders = bound.shape[0]
    for hop_index in range(HOPS):
        if hop_index == HOPS - 1:
            gathered = lax.all_gather(jnp.concatenate([exported, part_labels], axis=0), "dom")
            halo_rows = gathered[:, :borders].reshape(n_dom * borders, width)
            all_labels = gathered[:, borders:]
        else:
            halo_rows = lax.all_gather(exported, "dom", axis=0, tiled=True)
        hop_now, exported = propagate(
            hop_now, halo_rows, tile_columns, tile_values, pick_boundary
        )
        moved[hop_index], exported = lax.optimization_barrier((moved[hop_index], exported))
        moved.append(exchange_rows(hop_now.reshape(n_rep, batch_rows, width)))

    own_labels = lax.dynamic_index_in_dim(
        all_labels.reshape(n_dom, n_dom, train_dev // n_dom),
        lax.axis_index("dom"),
        axis=1,
        keepdims=False,
    ).reshape(train_dev).astype(jnp.int32)
    picked_rows = look_up(train_rows[0], shuffle[0]) - lax.axis_index("rep") * batch_rows
    paper_hot = (
        picked_rows == jnp.arange(batch_rows, dtype=jnp.int32)[None, :]
    ).astype(jnp.bfloat16)
    label_hot = (own_labels[:, None] == jnp.arange(classes, dtype=jnp.int32)[None, :]).astype(
        jnp.bfloat16
    )
    counts = outer_rows(paper_hot, label_hot)
    times = jnp.sum(counts, axis=1, keepdims=True)

    pre_first = None
    columns = []
    for hop_index in range(hop_count):
        part = moved[hop_index].transpose(1, 0, 2).reshape(batch_rows, n_rep * width)
        columns.append(part)
        weight = first_weight[:, hop_index * width : (hop_index + 1) * width].reshape(
            n_rep * width, hidden
        )
        term = jnp.dot(part, weight, preferred_element_type=jnp.float32)
        pre_first = term if pre_first is None else pre_first + term
    act_first, slope_first = gelu_pair(pre_first)
    act_first = act_first.astype(jnp.bfloat16)
    pre_mid = jnp.dot(act_first, mid_weight, preferred_element_type=jnp.float32)
    act_mid, slope_mid = gelu_pair(pre_mid)
    act_mid = act_mid.astype(jnp.bfloat16)
    logits = jnp.dot(act_mid, out_weight, preferred_element_type=jnp.float32)
    exp_logits = jnp.exp(logits)
    softmax_out = exp_logits / jnp.sum(exp_logits, axis=1, keepdims=True)
    grad_logits = jnp.where(times > 0.0, softmax_out * times - counts, 0.0)
    grad_logits = (grad_logits * (1.0 / math.sqrt(n_dom * train_dev))).astype(jnp.bfloat16)
    grad_mid = (inner_cols(grad_logits, out_weight) * slope_mid).astype(jnp.bfloat16)

    dom_bits = n_dom.bit_length() - 1
    quarter = hop_count * width // n_dom
    strip = hidden // (n_dom * n_rep)

    out_share = outer_rows(act_mid, grad_logits).astype(jnp.bfloat16)
    out_pad = -classes % 256
    out_share = jnp.pad(out_share, ((0, 0), (0, out_pad)))
    mid_share = outer_rows(act_first, grad_mid).astype(jnp.bfloat16)
    upper = jnp.concatenate([mid_share, out_share], axis=1)
    upper = upper.reshape(n_dom // 2, 2, n_rep, strip, hidden + classes + out_pad)
    upper = halve(upper, "dom", 0, 1).astype(jnp.bfloat16)
    upper = scatter_two_ways(upper.transpose(1, 0, 2, 3), dom_bits)

    grad_first = (inner_cols(grad_mid, mid_weight) * slope_first).astype(jnp.bfloat16)
    first_parts = []
    for part in columns:
        piece = outer_rows(part, grad_first).astype(jnp.bfloat16)
        piece = piece.reshape(n_rep, n_dom // (2 * hop_count), 2, quarter, hidden)
        first_parts.append(halve(piece, "dom", 0, 2).astype(jnp.bfloat16))
    lower = scatter_two_ways(jnp.concatenate(first_parts, axis=1), dom_bits)
    return (
        lower.reshape(1, quarter, hidden),
        upper[:, :hidden],
        upper[:, hidden : hidden + classes],
    )


def solution(mesh):
    placed = (
        P("dom", "rep"),
        P("dom", None, None, None),
        P("dom", None),
        P("dom", None),
        P("dom", None),
        P("dom", None),
        P(("dom", "rep")),
        P(),
        P(),
        P(),
    )
    return jax.shard_map(
        per_device,
        mesh=mesh,
        in_specs=placed,
        out_specs=(P("rep", "dom", None), P(("dom", "rep"), None), P(("dom", "rep"), None)),
        check_vma=False,
    )
```

```python
import functools
import math

import jax
import jax.numpy as jnp
from jax import lax
from jax.experimental import pallas as pl
from jax.experimental.pallas import tpu as pltpu
from jax.sharding import PartitionSpec as P

HOPS = 3
STEP_BLOCKS = 8

root_two_pi = 0.7978845608028654
cubic_term = 0.044715


def gelu_pair(values):
    inner_arg = root_two_pi * (values + cubic_term * values * values * values)
    tanh_part = jnp.tanh(inner_arg)
    output = 0.5 * values * (1.0 + tanh_part)
    slope_out = 0.5 * (1.0 + tanh_part) + 0.5 * values * (
        1.0 - tanh_part * tanh_part
    ) * root_two_pi * (1.0 + 3.0 * cubic_term * values * values)
    return (output, slope_out)


def outer_rows(left_side, right_side):
    return lax.dot_general(
        left_side, right_side, (((0,), (0,)), ((), ())), preferred_element_type=jnp.float32
    )


def inner_cols(left_side, right_side):
    return lax.dot_general(
        left_side, right_side, (((1,), (1,)), ((), ())), preferred_element_type=jnp.float32
    )


def hop_kernel(columns, hop_ref, halo_ref, tiles_ref, pick_ref, out_ref, export_ref, joined, total):
    step = pl.program_id(0)
    own_rows = hop_ref.shape[0]
    _, fan_in, tile, _ = tiles_ref.shape

    @pl.when(step == 0)
    def _():
        joined[:own_rows] = hop_ref[...]
        joined[own_rows:] = halo_ref[...]
        total[...] = jnp.zeros_like(total)

    for block in range(STEP_BLOCKS):
        row = step * STEP_BLOCKS + block
        left = jnp.concatenate([tiles_ref[block, k] for k in range(fan_in)], axis=1)
        right = jnp.concatenate(
            [
                joined[pl.ds(pl.multiple_of(columns[row, k] * tile, tile), tile)]
                for k in range(fan_in)
            ],
            axis=0,
        )
        summed = jnp.dot(left, right, preferred_element_type=jnp.float32)
        out_ref[block * tile : (block + 1) * tile] = summed.astype(out_ref.dtype)
    total[...] += jnp.dot(pick_ref[...], out_ref[...], preferred_element_type=jnp.float32)

    @pl.when(step == pl.num_programs(0) - 1)
    def _():
        export_ref[...] = total[...].astype(export_ref.dtype)


def propagate(hop_now, halo_rows, tile_columns, tile_values, pick_boundary):
    rows, width = hop_now.shape
    blocks, fan_in, tile, _ = tile_values.shape
    exported = pick_boundary.shape[0]
    step_rows = STEP_BLOCKS * tile
    whole = lambda step, columns: (0, 0)
    return pl.pallas_call(
        hop_kernel,
        grid_spec=pltpu.PrefetchScalarGridSpec(
            num_scalar_prefetch=1,
            grid=(blocks // STEP_BLOCKS,),
            in_specs=[
                pl.BlockSpec((rows, width), whole),
                pl.BlockSpec(halo_rows.shape, whole),
                pl.BlockSpec(
                    (STEP_BLOCKS, fan_in, tile, tile), lambda step, columns: (step, 0, 0, 0)
                ),
                pl.BlockSpec((exported, step_rows), lambda step, columns: (0, step)),
            ],
            out_specs=[
                pl.BlockSpec((step_rows, width), lambda step, columns: (step, 0)),
                pl.BlockSpec((exported, width), whole),
            ],
            scratch_shapes=[
                pltpu.VMEM((rows + halo_rows.shape[0], width), jnp.bfloat16),
                pltpu.VMEM((exported, width), jnp.float32),
            ],
        ),
        out_shape=[
            jax.ShapeDtypeStruct((rows, width), jnp.bfloat16),
            jax.ShapeDtypeStruct((exported, width), jnp.bfloat16),
        ],
        compiler_params=pltpu.CompilerParams(vmem_limit_bytes=40 * 1024 * 1024),
        cost_estimate=pl.CostEstimate(
            flops=2 * blocks * fan_in * tile * tile * width,
            bytes_accessed=2 * (tile_values.size + 4 * rows * width),
            transcendentals=0,
        ),
        name="propagate_hop",
    )(tile_columns, hop_now, halo_rows, tile_values, pick_boundary)


def exchange_rows(sent):
    return lax.all_to_all(sent, "rep", split_axis=0, concat_axis=0, tiled=True)


def halve(part, name, bit, axis):
    size = lax.axis_size(name)
    mine = (lax.axis_index(name) >> bit) & 1
    kept = lax.dynamic_index_in_dim(part, mine, axis, keepdims=False)
    sent = lax.dynamic_index_in_dim(part, 1 - mine, axis, keepdims=False)
    pairs = [(i, i ^ (1 << bit)) for i in range(size)]
    came = lax.ppermute(sent, name, pairs)
    return kept.astype(jnp.float32) + came.astype(jnp.float32)


def scatter_sum(part, bits, order, held=None):
    rows, cols = part.shape[-2:]
    left = list(bits)
    for bit in order:
        axis = 1 + left.index(bit)
        part = halve(part, "dom", bit, axis).astype(jnp.bfloat16)
        left.remove(bit)
        if held and bit == order[0]:
            part, held[0] = lax.optimization_barrier((part, held[0]))
    rep_bits = part.shape[0].bit_length() - 1
    part = part.reshape((2,) * rep_bits + (rows, cols))
    for bit in range(rep_bits):
        part = part.astype(jnp.bfloat16)
        part = halve(part, "rep", bit, rep_bits - 1 - bit)
    return part


def scatter_two_ways(part, dom_bits, held=None):
    n_rep, _, rows, cols = part.shape
    bits = list(range(dom_bits - 1, 0, -1))
    part = part.reshape((n_rep,) + (2,) * len(bits) + (rows, cols))
    rest = bits[::-1]
    middle = len(rest) // 2
    shares = [
        scatter_sum(part[..., : cols // 2], bits, rest, held),
        scatter_sum(part[..., cols // 2 :], bits, rest[middle:] + rest[:middle], held),
    ]
    return jnp.concatenate(shares, axis=-1)


def look_up(table, places):
    side = 64
    cells = table.reshape(-1, side)
    parts = jnp.concatenate([cells // side, cells % side], axis=1).astype(jnp.bfloat16)
    lines = jnp.arange(cells.shape[0], dtype=jnp.int32)
    line_hot = ((places // side)[:, None] == lines[None, :]).astype(jnp.bfloat16)
    found = jnp.dot(line_hot, parts, preferred_element_type=jnp.float32)
    found = found[:, :side] * side + found[:, side:]
    own = (places % side)[:, None] == jnp.arange(side, dtype=jnp.int32)[None, :]
    return jnp.sum(jnp.where(own, found, 0.0), axis=1, keepdims=True).astype(jnp.int32)


def per_device(
    features,
    tile_values,
    tile_columns,
    boundary_rows,
    train_rows,
    shuffle,
    labels,
    first_weight,
    mid_weight,
    out_weight,
):
    n_dom = lax.axis_size("dom")
    n_rep = lax.axis_size("rep")
    rows, width = features.shape
    train_dev = shuffle.shape[1]
    batch_rows = rows // n_rep
    hidden = mid_weight.shape[0]
    classes = out_weight.shape[1]
    hop_count = HOPS + 1

    bound = boundary_rows[0]
    pick_boundary = (bound[:, None] == jnp.arange(rows, dtype=jnp.int32)[None, :]).astype(
        jnp.bfloat16
    )

    label_rows = labels.astype(jnp.bfloat16).reshape(-1, width)
    lines = label_rows.shape[0]
    label_rows = jnp.concatenate([label_rows, label_rows], axis=0)
    riders = jnp.broadcast_to(label_rows[None], (n_rep,) + label_rows.shape)
    hop_now = features
    exported = features[bound]
    first_rows = exchange_rows(
        jnp.concatenate([hop_now.reshape(n_rep, batch_rows, width), riders], axis=1)
    )
    moved = [first_rows[:, :batch_rows]]
    part_labels = first_rows[:, batch_rows : batch_rows + lines].reshape(n_rep * lines, width)
    borders = bound.shape[0]
    for hop_index in range(HOPS):
        if hop_index == HOPS - 1:
            gathered = lax.all_gather(jnp.concatenate([exported, part_labels], axis=0), "dom")
            halo_rows = gathered[:, :borders].reshape(n_dom * borders, width)
            all_labels = gathered[:, borders:]
        else:
            halo_rows = lax.all_gather(exported, "dom", axis=0, tiled=True)
        hop_now, exported = propagate(
            hop_now, halo_rows, tile_columns, tile_values, pick_boundary
        )
        moved[hop_index], exported = lax.optimization_barrier((moved[hop_index], exported))
        moved.append(exchange_rows(hop_now.reshape(n_rep, batch_rows, width)))

    own_labels = lax.dynamic_index_in_dim(
        all_labels.reshape(n_dom, n_dom, train_dev // n_dom),
        lax.axis_index("dom"),
        axis=1,
        keepdims=False,
    ).reshape(train_dev).astype(jnp.int32)
    picked_rows = look_up(train_rows[0], shuffle[0]) - lax.axis_index("rep") * batch_rows
    paper_hot = (
        picked_rows == jnp.arange(batch_rows, dtype=jnp.int32)[None, :]
    ).astype(jnp.bfloat16)
    label_hot = (own_labels[:, None] == jnp.arange(classes, dtype=jnp.int32)[None, :]).astype(
        jnp.bfloat16
    )
    counts = outer_rows(paper_hot, label_hot)
    times = jnp.sum(counts, axis=1, keepdims=True)

    pre_first = None
    columns = []
    for hop_index in range(hop_count):
        part = moved[hop_index].transpose(1, 0, 2).reshape(batch_rows, n_rep * width)
        columns.append(part)
        weight = first_weight[:, hop_index * width : (hop_index + 1) * width].reshape(
            n_rep * width, hidden
        )
        term = jnp.dot(part, weight, preferred_element_type=jnp.float32)
        pre_first = term if pre_first is None else pre_first + term
    act_first, slope_first = gelu_pair(pre_first)
    act_first = act_first.astype(jnp.bfloat16)
    pre_mid = jnp.dot(act_first, mid_weight, preferred_element_type=jnp.float32)
    act_mid, slope_mid = gelu_pair(pre_mid)
    act_mid = act_mid.astype(jnp.bfloat16)
    logits = jnp.dot(act_mid, out_weight, preferred_element_type=jnp.float32)
    exp_logits = jnp.exp(logits)
    softmax_out = exp_logits / jnp.sum(exp_logits, axis=1, keepdims=True)
    grad_logits = jnp.where(times > 0.0, softmax_out * times - counts, 0.0)
    grad_logits = (grad_logits * (1.0 / math.sqrt(n_dom * train_dev))).astype(jnp.bfloat16)
    grad_mid = (inner_cols(grad_logits, out_weight) * slope_mid).astype(jnp.bfloat16)

    dom_bits = n_dom.bit_length() - 1
    quarter = hop_count * width // n_dom
    strip = hidden // (n_dom * n_rep)

    out_share = outer_rows(act_mid, grad_logits).astype(jnp.bfloat16)
    out_pad = -classes % 256
    out_share = jnp.pad(out_share, ((0, 0), (0, out_pad)))
    mid_share = outer_rows(act_first, grad_mid).astype(jnp.bfloat16)
    upper = jnp.concatenate([mid_share, out_share], axis=1)
    upper = upper.reshape(n_dom // 2, 2, n_rep, strip, hidden + classes + out_pad)
    upper = halve(upper, "dom", 0, 1).astype(jnp.bfloat16)
    grad_first = (inner_cols(grad_mid, mid_weight) * slope_first).astype(jnp.bfloat16)
    held = [grad_first]
    upper = scatter_two_ways(upper.transpose(1, 0, 2, 3), dom_bits, held)
    first_parts = []
    for hop_index, part in enumerate(columns):
        late = hop_index >= hop_count // 2
        piece = outer_rows(part, held[0] if late else grad_first).astype(jnp.bfloat16)
        piece = piece.reshape(n_rep, n_dom // (2 * hop_count), 2, quarter, hidden)
        first_parts.append(halve(piece, "dom", 0, 2).astype(jnp.bfloat16))
    lower = scatter_two_ways(jnp.concatenate(first_parts, axis=1), dom_bits)
    return (
        lower.reshape(1, quarter, hidden),
        upper[:, :hidden],
        upper[:, hidden : hidden + classes],
    )


def solution(mesh):
    placed = (
        P("dom", "rep"),
        P("dom", None, None, None),
        P("dom", None),
        P("dom", None),
        P("dom", None),
        P("dom", None),
        P(("dom", "rep")),
        P(),
        P(),
        P(),
    )
    return jax.shard_map(
        per_device,
        mesh=mesh,
        in_specs=placed,
        out_specs=(P("rep", "dom", None), P(("dom", "rep"), None), P(("dom", "rep"), None)),
        check_vma=False,
    )
```
